128 devices in a mesh: dp: 32 (over z_hi, y, x), mp: 4 (over z_lo, core).
Axes of the slice: x: 4, y: 4, z: 4 (z_hi: 2, z_lo: 2; z = z_hi * 2 + z_lo), core: 2. Of those that a mesh axis runs over, the one named last changes fastest.
Arguments:
- attention: bfloat16 [16384, 2048], P('dp', 'mp')
- out_proj: bfloat16 [2048, 5376], P('mp'), may hold values from -0.125 to 0.125
- post_gain: float32 [5376], replicated, may hold values from 0.5 to 1.5
- residual: bfloat16 [16384, 5376], P('dp', 'mp'), may hold values from -6 to 6
- cotangent: bfloat16 [16384, 5376], P('dp', 'mp'), may hold values from -6 to 6
- counted: int32 [30], replicated, may hold values from 0 to 31, as said below
- master: float32 [4, 512, 5376], P('mp', 'dp'), may hold values from -0.125 to 0.125
- moment: float32 [4, 512, 5376], P('mp', 'dp'), may hold values from -12 to 12
- second: float32 [4, 512, 5376], P('mp', 'dp'), may hold values from 1 to 100
Outputs:
- layer_out: bfloat16 [16384, 5376], P('dp', 'mp')
- attn_grad: bfloat16 [16384, 2048], P('dp', 'mp')
- new_proj: bfloat16 [2048, 5376], P('mp')
- new_master: float32 [4, 512, 5376], P('mp', 'dp')
- new_moment: float32 [4, 512, 5376], P('mp', 'dp')
- new_second: float32 [4, 512, 5376], P('mp', 'dp')
The draws below stay inside these ranges and needn't reach their ends.
Inputs may be any that keep to these rules, and one draw needn't show every extreme that they name: 30 distinct replica indices; the first and the last replica are always counted.
All inputs are finite; a program needn't handle non-finite values.
Results may differ from the reference program's by a relative error of at most 0.0049.
Values may be sent and summed in bfloat16 or wider, within the bound.
No kernel may reach another device: no remote copies, remote signals or barrier semaphores. Data moves between devices by JAX's collectives and lax.ppermute only.
A program may use at most 128 MiB of HBM per device.

```python
import math
import jax
import jax.numpy as jnp
from jax import lax

D = 5376
TOK_DEV = 512
BACKUP = 2
HD = 2048
HL = 512
TOKENS = 16384
COUNTED = 30
N_DP = 32
N_MP = 4


def draw_attention(key, part):
    key = jax.random.fold_in(key, 11)
    keys = jax.random.split(key, 3)
    row_scale = jnp.exp(jax.random.uniform(keys[0], (TOKENS, 1), minval=0.0, maxval=math.log(10.0)))
    col_scale = jnp.exp(jax.random.uniform(keys[1], (1, HD), minval=math.log(0.3), maxval=math.log(3.0)))
    base = jax.random.normal(keys[2], (TOKENS, HD))
    return (0.5 * base * row_scale * col_scale).astype(jnp.float32).astype(jnp.bfloat16)


def draw_counted(key, part):
    key = jax.random.fold_in(key, 7)
    middle = jax.random.permutation(key, N_DP - 2) + 1
    ends = jnp.array([0, N_DP - 1], dtype=jnp.int32)
    return jnp.concatenate([ends, middle[BACKUP:].astype(jnp.int32)])


def block_levels(own_key, shape, pieces, least, top_value):
    factor_of = 1.0
    for dim, shards_of in pieces:
        steps = jax.random.uniform(jax.random.fold_in(jax.random.fold_in(own_key, 6), dim), (shards_of,), jnp.float32, least / len(pieces), top_value / len(pieces))
        factor_of = factor_of * jnp.repeat(jnp.exp(steps), shape[dim] // shards_of).reshape((-1,) + (1,) * (len(shape) - 1 - dim))
    return factor_of


def scatter_about(key, extent, scale, most, pieces=(), kind=jnp.bfloat16):
    drawn = jax.random.normal(key, extent, jnp.float32) * scale
    if len(pieces) > 0:
        drawn = block_levels(key, extent, pieces, -0.22, 0.18) * drawn
    return jnp.clip(drawn, min=-most, max=most).astype(kind)


def setup_inputs(seed: int = 0) -> dict:
    splits = jax.random.split(jax.random.key(seed), 10)
    return {
        "attention": draw_attention(jax.random.fold_in(splits[9], 71), 0),
        "out_proj": scatter_about(splits[1], (HD, D), HD ** -0.5, 0.125, ((0, 4),)),
        "post_gain": jnp.clip(1.0 + 0.1 * jax.random.normal(splits[2], (D,), jnp.float32), 0.5, 1.5),
        "residual": scatter_about(splits[3], (TOKENS, D), 1.0, 6.0, ((0, 32), (1, 4))),
        "cotangent": scatter_about(splits[4], (TOKENS, D), 1.0, 6.0, ((0, 32), (1, 4))),
        "counted": draw_counted(jax.random.fold_in(splits[9], 71), 0),
        "master": scatter_about(splits[6], (N_MP, HL, D), HD ** -0.5, 0.125, ((0, 4), (1, 32)), jnp.float32),
        "moment": scatter_about(splits[7], (N_MP, HL, D), 2.0, 12.0, ((0, 4), (1, 32)), jnp.float32),
        "second": jnp.clip(jnp.exp(math.log(100.0) - 4.6051702 * jax.random.uniform(splits[8], (N_MP, HL, D), jnp.float32) ** block_levels(splits[8], (N_MP, HL, D), ((0, 4), (1, 32)), -0.2, 0.2)), 1.0, 100.0),
    }


norm_eps = 1e-06
beta_one = 0.9
beta_two = 0.999
adam_eps = 1e-08
learn_rate = 0.01
weight_decay = 0.1
step_number = 100.0

def reference(attention, out_proj, post_gain, residual, cotangent, counted, master, moment, second):
    pre = jnp.dot(attention, out_proj, preferred_element_type=jnp.float32)
    inv_rms = lax.rsqrt(lax.optimization_barrier(jnp.mean(pre * pre, axis=1, keepdims=True)) + norm_eps)
    layer_out = (residual.astype(jnp.float32) + post_gain[None, :] * (pre * inv_rms)).astype(jnp.bfloat16)
    scaled = cotangent.astype(jnp.float32) * post_gain[None, :]
    proj = lax.optimization_barrier(jnp.mean(scaled * pre, axis=1, keepdims=True))
    pre_grad = (inv_rms * scaled - pre * inv_rms ** 3 * proj).astype(jnp.bfloat16)
    attn_grad = lax.dot_general(pre_grad, out_proj, (((1,), (1,)), ((), ())), preferred_element_type=jnp.float32).astype(jnp.bfloat16)
    replica_ids = jnp.arange(TOKENS, dtype=jnp.int32) // TOK_DEV
    counted_flag = lax.optimization_barrier(jnp.sum((counted[None, :] == replica_ids[:, None]).astype(jnp.float32), axis=1))
    masked = (attention.astype(jnp.float32) * counted_flag[:, None]).astype(jnp.bfloat16)
    summed = lax.dot_general(masked, pre_grad, (((0,), (0,)), ((), ())), preferred_element_type=jnp.float32)
    mean_grad = (summed / COUNTED).reshape(N_MP, HL, D)
    new_moment = beta_one * moment + (1.0 - beta_one) * mean_grad
    new_second = beta_two * second + (1.0 - beta_two) * mean_grad * mean_grad
    update = new_moment / (1.0 - beta_one ** step_number) / (jnp.sqrt(new_second / (1.0 - beta_two ** step_number)) + adam_eps)
    new_master = master - learn_rate * (update + weight_decay * master)
    new_proj = new_master.reshape(HD, D).astype(jnp.bfloat16)
    return (layer_out, attn_grad, new_proj, new_master, new_moment, new_second)
```

```python
import jax
import jax.numpy as jnp
from jax import lax
from jax.sharding import Mesh, PartitionSpec as P

norm_eps = 1e-06
beta_one = 0.9
beta_two = 0.999
adam_eps = 1e-08
learn_rate = 0.01
weight_decay = 0.1
step_number = 100.0

axes = ("zh", "y", "x", "zl", "c")
bf16 = jnp.bfloat16
f32 = jnp.float32


def pick(stacked, index, axis=0):
    return lax.dynamic_index_in_dim(stacked, index, axis, keepdims=False)


def ring_step(value, axis, step):
    size = 4
    return lax.ppermute(value, axis, [(i, (i + step) % size) for i in range(size)])


def flip(value, axis):
    return lax.ppermute(value, axis, [(0, 1), (1, 0)])


def flip_mp(value, bits):
    return lax.ppermute(value, ("zl", "c"), [(i, i ^ bits) for i in range(4)])


def ring_sum(pieces, axis):
    place = lax.axis_index(axis)
    dim = {"y": 2, "x": 3}[axis]
    dim = min(dim, pieces.ndim - 3)
    got = [ring_step(pick(pieces, (place + s) % 4, dim), axis, s) for s in (2, 1, 3)]
    total = pick(pieces, place, dim).astype(f32)
    for one in got:
        total = total + one.astype(f32)
    return total.astype(bf16)


def local(attention, out_proj, post_gain, residual, cotangent, counted, master, moment, second):
    zh, y, x, zl, c = (lax.axis_index(a) for a in axes)
    place = zl * 2 + c
    replica = (zh * 4 + y) * 4 + x
    tokens, part_width = residual.shape
    heads = attention.shape[1]
    full_width = post_gain.shape[0]
    gain_part = lax.dynamic_slice_in_dim(post_gain, place * part_width, part_width, 0)[None, :]
    counted_flag = jnp.sum((counted == replica).astype(f32))

    columns = jnp.stack([out_proj[:, j * part_width : (j + 1) * part_width] for j in range(4)])
    columns = lax.optimization_barrier(columns)
    weights = [
        pick(columns, place),
        flip(pick(columns, place ^ 1), "c"),
        lax.ppermute(
            pick(columns, place ^ 2), ("zh", "zl"), [(i, (i + 1) % 4) for i in range(4)]
        ),
        lax.ppermute(
            pick(columns, place ^ 3),
            ("zh", "zl", "c"),
            [(i * 2 + j, ((i + 3) % 4) * 2 + 1 - j) for i in range(4) for j in range(2)],
        ),
    ]
    far = flip(attention, "zl")
    near = flip(attention, "c")
    features = [attention, near, far, flip(far, "c")]

    pre = 0.0
    for feature, weight in zip(features, weights):
        pre = pre + jnp.dot(feature, weight, preferred_element_type=f32)
    scaled = cotangent.astype(f32) * gain_part
    stats = jnp.stack([jnp.sum(pre * pre, axis=1), jnp.sum(scaled * pre, axis=1)])
    stats = stats + flip(stats, "c")
    stats = stats + flip(stats, "zl")
    inv_rms = lax.rsqrt(stats[0] / full_width + norm_eps)[:, None]
    proj = (stats[1] / full_width)[:, None]
    layer_out = (residual.astype(f32) + gain_part * (pre * inv_rms)).astype(bf16)
    pre_grad = (inv_rms * scaled - pre * inv_rms**3 * proj).astype(bf16)

    halves = []
    for pair in (0, 2):
        left = jnp.concatenate([features[pair], features[pair + 1]], axis=1)
        left = (left.astype(f32) * counted_flag).astype(bf16)
        term = lax.dot_general(left, pre_grad, (((0,), (0,)), ((), ())), preferred_element_type=f32)
        halves.append(term.astype(bf16).reshape(2, 2, 4, 4, 16, part_width))
    first = ring_sum(halves[0], "x")
    second_half = ring_sum(halves[1], "y")
    first = ring_sum(first, "y")
    second_half = ring_sum(second_half, "x")
    both = jnp.concatenate([first, second_half])
    gathered = []
    for k in range(4):
        mine = []
        for h in range(2):
            block = pick(both[k], zh ^ h)
            if h == 0 and k == 0:
                mine.append(block.astype(f32))
                continue
            moves = [
                (((i * 2 + j) * 2 + l), ((i ^ h) * 2 + (j ^ (k >> 1))) * 2 + (l ^ (k & 1)))
                for i in range(2)
                for j in range(2)
                for l in range(2)
            ]
            mine.append(lax.ppermute(block, ("zh", "zl", "c"), moves).astype(f32))
        gathered.append(mine[0] + mine[1])
    gathered = jnp.stack(gathered)
    owned_sum = jnp.concatenate([pick(gathered, place ^ j) for j in range(4)], axis=1)

    mean_grad = (owned_sum / counted.shape[0])[None, :, :]
    new_moment = beta_one * moment + (1.0 - beta_one) * mean_grad
    new_second = beta_two * second + (1.0 - beta_two) * mean_grad * mean_grad
    update = (
        new_moment
        / (1.0 - beta_one**step_number)
        / (jnp.sqrt(new_second / (1.0 - beta_two**step_number)) + adam_eps)
    )
    new_master = master - learn_rate * (update + weight_decay * master)

    own = new_master[0].astype(bf16)
    other = flip(own, "zh")
    rows = jnp.where(zh == 0, jnp.stack([own, other]), jnp.stack([other, own]))
    cut = full_width // 2
    parts = []
    for order, piece in ((("y", "x"), rows[:, :, :cut]), (("x", "y"), rows[:, :, cut:])):
        for axis in order:
            spot = lax.axis_index(axis)
            stacked = jnp.stack([piece] + [ring_step(piece, axis, s) for s in (1, 2, 3)])
            piece = jnp.stack([pick(stacked, (spot - j) % 4) for j in range(4)])
        parts.append(piece)
    left_cols = jnp.transpose(parts[0], (2, 1, 0, 3, 4))
    right_cols = jnp.transpose(parts[1], (2, 0, 1, 3, 4))
    new_proj = jnp.concatenate([left_cols, right_cols], axis=-1).reshape(heads, full_width)

    partial = [
        lax.dot_general(pre_grad, w, (((1,), (1,)), ((), ())), preferred_element_type=f32)
        for w in weights
    ]
    attn_grad = partial[0]
    for k in (1, 2, 3):
        attn_grad = attn_grad + flip_mp(partial[k].astype(bf16), k).astype(f32)
    return (layer_out, attn_grad.astype(bf16), new_proj, new_master, new_moment, new_second)


def solution(mesh):
    wide = Mesh(mesh.devices.reshape(2, 4, 4, 2, 2), axes)
    dp, mp = ("zh", "y", "x"), ("zl", "c")
    return jax.shard_map(
        local,
        mesh=wide,
        in_specs=(
            P(dp, mp),
            P(mp, None),
            P(),
            P(dp, mp),
            P(dp, mp),
            P(),
            P(mp, dp, None),
            P(mp, dp, None),
            P(mp, dp, None),
        ),
        out_specs=(
            P(dp, mp),
            P(dp, mp),
            P(mp, None),
            P(mp, dp, None),
            P(mp, dp, None),
            P(mp, dp, None),
        ),
        check_vma=False,
    )
```

```python
import jax
import jax.numpy as jnp
from jax import lax
from jax.experimental import pallas as pl
from jax.experimental.pallas import tpu as pltpu
from jax.sharding import Mesh, PartitionSpec as P

norm_eps = 1e-06
beta_one = 0.9
beta_two = 0.999
adam_eps = 1e-08
learn_rate = 0.01
weight_decay = 0.1
step_number = 100.0

axes = ("zh", "y", "x", "zl", "c")
sizes = (2, 4, 4, 2, 2)
bf16 = jnp.bfloat16
f32 = jnp.float32

places = [
    (zh, y, x, zl, c)
    for zh in range(2)
    for y in range(4)
    for x in range(4)
    for zl in range(2)
    for c in range(2)
]


def move(value, target):
    def flat(place):
        index = 0
        for size, at in zip(sizes, place):
            index = index * size + at % size
        return index

    return lax.ppermute(value, axes, [(flat(p), flat(target(*p))) for p in places])


def along_first(value, step):
    return move(
        value,
        lambda zh, y, x, zl, c: (zh, y, x + step, zl, c) if c == 0 else (zh, y + step, x, zl, c),
    )


def along_second(value, step):
    return move(
        value,
        lambda zh, y, x, zl, c: (zh, y + step, x, zl, c) if c == 0 else (zh, y, x + step, zl, c),
    )


def flip_core(value):
    return move(value, lambda zh, y, x, zl, c: (zh, y, x, zl, 1 - c))


def flip_z(value, low, high):
    return move(value, lambda zh, y, x, zl, c: (zh ^ high, y, x, zl ^ low, c))


def gradient_kernel(rows_ref, left_ref, own_ref, peer_ref, *rest):
    outs, (both, sent, sems) = rest[:4], rest[4:]
    step = pl.program_id(0)
    part = own_ref.shape[0]
    width = outs[0].shape[-1]

    @pl.when(step == 0)
    def _():
        core = rows_ref[64]
        first = pltpu.make_async_copy(
            own_ref, both.at[pl.ds(pl.multiple_of(core * part, 64), part)], sems.at[0]
        )
        second = pltpu.make_async_copy(
            peer_ref, both.at[pl.ds(pl.multiple_of((1 - core) * part, 64), part)], sems.at[1]
        )
        first.start()
        second.start()
        for k in range(64):
            row = pl.multiple_of(rows_ref[k], 16)
            sent[pl.ds(16 * k, 16), :] = left_ref[pl.ds(row, 16), :]
        first.wait()
        second.wait()

    block = both[pl.ds(pl.multiple_of(step * width, width), width), :]
    for s in range(4):
        term = lax.dot_general(
            sent[pl.ds(256 * s, 256), :],
            block,
            (((1,), (1,)), ((), ())),
            preferred_element_type=f32,
        )
        outs[s][...] = term.astype(bf16).reshape(16, 16, width)


def gradient_pieces(rows, left, own, peer):
    heads, tokens = left.shape
    part = own.shape[0]
    width = 384
    columns = 2 * part
    return pl.pallas_call(
        gradient_kernel,
        grid_spec=pltpu.PrefetchScalarGridSpec(
            num_scalar_prefetch=1,
            grid=(columns // width,),
            in_specs=[
                pl.BlockSpec((heads, tokens), lambda i, rows: (0, 0)),
                pl.BlockSpec(memory_space=pl.ANY),
                pl.BlockSpec(memory_space=pl.ANY),
            ],
            out_specs=[pl.BlockSpec((16, 16, width), lambda i, rows: (0, 0, i))] * 4,
            scratch_shapes=[
                pltpu.VMEM((columns, tokens), bf16),
                pltpu.VMEM((heads, tokens), bf16),
                pltpu.SemaphoreType.DMA((2,)),
            ],
        ),
        out_shape=[jax.ShapeDtypeStruct((16, 16, columns), bf16)] * 4,
        compiler_params=pltpu.CompilerParams(vmem_limit_bytes=32 * 1024 * 1024),
        cost_estimate=pl.CostEstimate(
            flops=2 * heads * tokens * columns, bytes_accessed=10_000_000, transcendentals=0
        ),
    )(rows, left, own, peer)


def join_kernel(*refs):
    *pieces, ready_ref, out_ref = refs
    size = pieces[0].shape[0]
    for t, piece in enumerate(pieces):
        out_ref[size * t : size * (t + 1)] = piece[...]


def join(pieces, ready):
    size, rows, width = pieces[0].shape
    vmem = pl.BlockSpec(memory_space=pltpu.VMEM)
    return pl.pallas_call(
        join_kernel,
        in_specs=[vmem] * (len(pieces) + 1),
        out_specs=vmem,
        out_shape=jax.ShapeDtypeStruct((len(pieces) * size, rows, width), bf16),
        compiler_params=pltpu.CompilerParams(vmem_limit_bytes=16 * 1024 * 1024),
        cost_estimate=pl.CostEstimate(flops=0, bytes_accessed=2_800_000, transcendentals=0),
    )(*pieces, ready)


def place_kernel(rows_ref, *refs):
    pieces, out_ref, sems = refs[:4], refs[4], refs[5]
    copies = [
        pltpu.make_async_copy(
            pieces[s].at[k],
            out_ref.at[pl.ds(pl.multiple_of(rows_ref[s * 8 + k], 16), 16)],
            sems.at[s * 8 + k],
        )
        for s in range(4)
        for k in range(8)
    ]
    for copy in copies:
        copy.start()
    for copy in copies:
        copy.wait()


def place_rows(rows, pieces):
    width = pieces[0].shape[-1]
    return pl.pallas_call(
        place_kernel,
        grid_spec=pltpu.PrefetchScalarGridSpec(
            num_scalar_prefetch=1,
            grid=(1,),
            in_specs=[pl.BlockSpec(memory_space=pltpu.VMEM)] * 4,
            out_specs=pl.BlockSpec(memory_space=pl.ANY),
            scratch_shapes=[pltpu.SemaphoreType.DMA((32,))],
        ),
        compiler_params=pltpu.CompilerParams(vmem_limit_bytes=24 * 1024 * 1024),
        out_shape=jax.ShapeDtypeStruct((512, width), bf16),
        cost_estimate=pl.CostEstimate(flops=0, bytes_accessed=11_000_000, transcendentals=0),
    )(rows, *pieces)


def local(attention, out_proj, post_gain, residual, cotangent, counted, master, moment, second):
    zh, y, x, zl, c = (lax.axis_index(a) for a in axes)
    replica = (zh * 4 + y) * 4 + x
    tokens, part = residual.shape
    heads = attention.shape[1]
    full_width = post_gain.shape[0]
    half = full_width // 2
    gain = lax.dynamic_slice_in_dim(post_gain, (zl * 2 + c) * part, part, 0)[:, None]
    counted_flag = jnp.sum((counted == replica).astype(f32))
    spot = jnp.where(c == 0, x, y)
    spot_second = jnp.where(c == 0, y, x)

    near = jnp.where(zl == 0, out_proj[:, :half], out_proj[:, half:])
    share, shared = 80, 320
    shares = lax.dynamic_slice_in_dim(out_proj, spot * share, share, 0)
    received = flip_z(jnp.where(zl == 0, shares[:, half:], shares[:, :half]), 1, 0)
    rest = out_proj[shared:]
    direct = flip_z(jnp.where(zl == 0, rest[:, half:], rest[:, :half]), 1, 1)
    far_attention = flip_z(attention, 1, 0)
    rel = jnp.stack([received] + [along_first(received, s) for s in (1, 2, 3)])
    far = jnp.concatenate(
        [lax.dynamic_index_in_dim(rel, (spot - j) % 4, 0, keepdims=False) for j in range(4)]
        + [direct]
    )

    left_rows = (((0,), (1,)), ((), ()))
    pre_pair = lax.dot_general(near, attention, left_rows, preferred_element_type=f32)
    pre_pair = pre_pair + lax.dot_general(far, far_attention, left_rows, preferred_element_type=f32)
    mine = lax.dynamic_slice_in_dim(pre_pair, c * part, part, 0)
    other = lax.dynamic_slice_in_dim(pre_pair, (1 - c) * part, part, 0)
    pre = mine + flip_core(other.astype(bf16)).astype(f32)

    scaled = cotangent.T.astype(f32) * gain
    stats = jnp.stack([jnp.sum(pre * pre, axis=0), jnp.sum(scaled * pre, axis=0)])
    stats = stats + flip_core(stats)
    stats = stats + flip_z(stats, 1, 0)
    inv_rms = lax.rsqrt(stats[0] / full_width + norm_eps)[None, :]
    proj = (stats[1] / full_width)[None, :]
    layer_out = (residual.T.astype(f32) + gain * (pre * inv_rms)).astype(bf16).T
    pre_grad = (inv_rms * scaled - pre * inv_rms**3 * proj).astype(bf16)
    peer_grad = flip_core(pre_grad)

    left = jnp.concatenate([attention, far_attention], axis=1)
    left = (left.astype(f32) * counted_flag).astype(bf16).T
    left = lax.optimization_barrier(left)
    s_, t_, slot_, dz_ = jnp.meshgrid(*(jnp.arange(n) for n in (4, 4, 2, 2)), indexing="ij")
    first_at = (spot + s_) % 4
    second_at = (spot_second + t_) % 4
    x_at = jnp.where(c == 0, first_at, second_at)
    y_at = jnp.where(c == 0, second_at, first_at)
    rows = slot_ * 512 + (((zh ^ dz_) * 4 + y_at) * 4 + x_at) * 16
    rows = jnp.concatenate([rows.reshape(64), c[None]]).astype(jnp.int32)
    pieces = gradient_pieces(rows, left, pre_grad, peer_grad)
    got = [along_first(pieces[s], s) for s in (2, 1, 3)]
    total = pieces[0].astype(f32)
    for one in got:
        total = total + one.astype(f32)
    total = total.astype(bf16).reshape(4, 4, 16, half)
    got = [along_second(total[t], t) for t in (2, 1, 3)]
    final = total[0].astype(f32)
    for one in got:
        final = final + one.astype(f32)
    final = final.astype(bf16).reshape(2, 2, 16, half)
    got = [flip_z(final[1, 1], 1, 1), flip_z(final[0, 1], 0, 1), flip_z(final[1, 0], 1, 0)]
    own_columns = final[0, 0].astype(f32) + got[1].astype(f32)
    far_columns = got[2].astype(f32) + got[0].astype(f32)
    owned_sum = jnp.where(
        zl == 0,
        jnp.concatenate([own_columns, far_columns], axis=1),
        jnp.concatenate([far_columns, own_columns], axis=1),
    )

    mean_grad = (owned_sum / counted.shape[0])[None, :, :]
    new_moment = beta_one * moment + (1.0 - beta_one) * mean_grad
    new_second = beta_two * second + (1.0 - beta_two) * mean_grad * mean_grad
    update = (
        new_moment
        / (1.0 - beta_one**step_number)
        / (jnp.sqrt(new_second / (1.0 - beta_two**step_number)) + adam_eps)
    )
    new_master = master - learn_rate * (update + weight_decay * master)

    own = new_master[0].astype(bf16)
    block = jnp.stack([own, flip_z(own, 0, 1)])
    got = [along_second(block, t) for t in (1, 2, 3)]
    block = join([block] + got, flip_core(jnp.concatenate([one[0, :, :128] for one in got])))
    spread = [block] + [along_first(block, s) for s in (1, 2, 3)]
    s_, t_, dz_ = jnp.meshgrid(*(jnp.arange(n) for n in (4, 4, 2)), indexing="ij")
    first_at = (spot - s_) % 4
    second_at = (spot_second - t_) % 4
    x_at = jnp.where(c == 0, first_at, second_at)
    y_at = jnp.where(c == 0, second_at, first_at)
    rows = ((((zh ^ dz_) * 4 + y_at) * 4 + x_at) * 16).reshape(32).astype(jnp.int32)
    new_proj = place_rows(rows, spread)

    pre_grad, peer_grad, _ = lax.optimization_barrier((pre_grad, peer_grad, pieces[0]))
    pair = jnp.stack([pre_grad, peer_grad])
    pair = jnp.concatenate(
        [lax.dynamic_index_in_dim(pair, c ^ j, 0, keepdims=False) for j in range(2)]
    )
    to_heads = (((0,), (1,)), ((), ()))
    attn_far = lax.dot_general(pair, far, to_heads, preferred_element_type=f32).astype(bf16)
    attn_near = lax.dot_general(pair, near, to_heads, preferred_element_type=f32)
    attn_grad = (attn_near + flip_z(attn_far, 1, 0).astype(f32)).astype(bf16)
    return (layer_out, attn_grad, new_proj, new_master, new_moment, new_second)


def solution(mesh):
    wide = Mesh(mesh.devices.reshape(sizes), axes)
    dp, mp = ("zh", "y", "x"), ("zl", "c")
    return jax.shard_map(
        local,
        mesh=wide,
        in_specs=(
            P(dp, mp),
            P(mp, None),
            P(),
            P(dp, mp),
            P(dp, mp),
            P(),
            P(mp, dp, None),
            P(mp, dp, None),
            P(mp, dp, None),
        ),
        out_specs=(
            P(dp, mp),
            P(dp, mp),
            P(mp, None),
            P(mp, dp, None),
            P(mp, dp, None),
            P(mp, dp, None),
        ),
        check_vma=False,
    )
```

```python
import jax
import jax.numpy as jnp
from jax import lax
from jax.experimental import pallas as pl
from jax.experimental.pallas import tpu as pltpu
from jax.sharding import Mesh, PartitionSpec as P

norm_eps = 1e-06
beta_one = 0.9
beta_two = 0.999
adam_eps = 1e-08
learn_rate = 0.01
weight_decay = 0.1
step_number = 100.0

axes = ("zh", "y", "x", "zl", "c")
sizes = (2, 4, 4, 2, 2)
bf16 = jnp.bfloat16
f32 = jnp.float32

places = [
    (zh, y, x, zl, c)
    for zh in range(2)
    for y in range(4)
    for x in range(4)
    for zl in range(2)
    for c in range(2)
]


def move(value, target):
    def flat(place):
        index = 0
        for size, at in zip(sizes, place):
            index = index * size + at % size
        return index

    return lax.ppermute(value, axes, [(flat(p), flat(target(*p))) for p in places])


def along_first(value, step):
    return move(
        value,
        lambda zh, y, x, zl, c: (zh, y, x + step, zl, c) if c == 0 else (zh, y + step, x, zl, c),
    )


def along_second(value, step):
    return move(
        value,
        lambda zh, y, x, zl, c: (zh, y + step, x, zl, c) if c == 0 else (zh, y, x + step, zl, c),
    )


def flip_core(value):
    return move(value, lambda zh, y, x, zl, c: (zh, y, x, zl, 1 - c))


def flip_z(value, low, high):
    return move(value, lambda zh, y, x, zl, c: (zh ^ high, y, x, zl ^ low, c))


def gradient_kernel(rows_ref, left_ref, right_ref, *rest):
    outs, sent = rest[:4], rest[4]

    @pl.when(pl.program_id(0) == 0)
    def _():
        for k in range(32):
            row = pl.multiple_of(rows_ref[k], 16)
            sent[pl.ds(16 * k, 16), :] = left_ref[pl.ds(row, 16), :]

    term = lax.dot_general(
        sent[...], right_ref[...], (((1,), (1,)), ((), ())), preferred_element_type=f32
    )
    term = term.astype(bf16).reshape(4, 8, 16, right_ref.shape[0])
    for one in range(4):
        outs[one][...] = term[one]


def gradient_pieces(rows, left, right):
    heads, tokens = left.shape
    columns = right.shape[0]
    width = 384
    return pl.pallas_call(
        gradient_kernel,
        grid_spec=pltpu.PrefetchScalarGridSpec(
            num_scalar_prefetch=1,
            grid=(columns // width,),
            in_specs=[
                pl.BlockSpec((heads, tokens), lambda i, rows: (0, 0)),
                pl.BlockSpec((width, tokens), lambda i, rows: (i, 0)),
            ],
            out_specs=[pl.BlockSpec((8, 16, width), lambda i, rows: (0, 0, i))] * 4,
            scratch_shapes=[pltpu.VMEM((512, tokens), bf16)],
        ),
        out_shape=[jax.ShapeDtypeStruct((8, 16, columns), bf16)] * 4,
        compiler_params=pltpu.CompilerParams(vmem_limit_bytes=24 * 1024 * 1024),
        cost_estimate=pl.CostEstimate(
            flops=2 * 512 * tokens * columns, bytes_accessed=6_000_000, transcendentals=0
        ),
    )(rows, left, right)


def place_kernel(rows_ref, *refs):
    *pieces, out_ref, sems = refs
    copies = [
        pltpu.make_async_copy(
            piece.at[k],
            out_ref.at[pl.ds(pl.multiple_of(rows_ref[4 * i + k], 16), 16)],
            sems.at[4 * i + k],
        )
        for i, piece in enumerate(pieces)
        for k in range(4)
    ]
    for copy in copies:
        copy.start()
    for copy in copies:
        copy.wait()


def place_more_kernel(rows_ref, earlier_ref, *refs):
    place_kernel(rows_ref, *refs)


def place_rows(rows, pieces, earlier=None):
    count = len(pieces)
    anywhere = pl.BlockSpec(memory_space=pl.ANY)
    before = [] if earlier is None else [earlier]
    return pl.pallas_call(
        place_more_kernel if before else place_kernel,
        grid_spec=pltpu.PrefetchScalarGridSpec(
            num_scalar_prefetch=1,
            grid=(1,),
            in_specs=[anywhere] * len(before) + [pl.BlockSpec(memory_space=pltpu.VMEM)] * count,
            out_specs=anywhere,
            scratch_shapes=[pltpu.SemaphoreType.DMA((4 * count,))],
        ),
        out_shape=jax.ShapeDtypeStruct((512, pieces[0].shape[-1]), bf16),
        input_output_aliases={1: 0} if before else {},
        compiler_params=pltpu.CompilerParams(vmem_limit_bytes=24 * 1024 * 1024),
        cost_estimate=pl.CostEstimate(
            flops=0, bytes_accessed=1_400_000 * count, transcendentals=0
        ),
    )(rows, *before, *pieces)


def local(attention, out_proj, post_gain, residual, cotangent, counted, master, moment, second):
    zh, y, x, zl, c = (lax.axis_index(a) for a in axes)
    replica = (zh * 4 + y) * 4 + x
    tokens, part = residual.shape
    heads = attention.shape[1]
    full_width = post_gain.shape[0]
    half = full_width // 2
    gain = lax.dynamic_slice_in_dim(post_gain, (zl * 2 + c) * part, part, 0)[:, None]
    counted_flag = jnp.sum((counted == replica).astype(f32))
    spot = jnp.where(c == 0, x, y)
    spot_second = jnp.where(c == 0, y, x)

    near = jnp.where(zl == 0, out_proj[:, :half], out_proj[:, half:])
    share, shared = 80, 320
    shares = lax.dynamic_slice_in_dim(out_proj, spot * share, share, 0)
    received = flip_z(jnp.where(zl == 0, shares[:, half:], shares[:, :half]), 1, 0)
    rest = out_proj[shared:]
    direct = flip_z(jnp.where(zl == 0, rest[:, half:], rest[:, :half]), 1, 1)
    far_attention = flip_z(attention, 1, 0)
    rel = jnp.stack([received] + [along_first(received, s) for s in (1, 2, 3)])
    far = jnp.concatenate(
        [lax.dynamic_index_in_dim(rel, (spot - j) % 4, 0, keepdims=False) for j in range(4)]
        + [direct]
    )

    left_rows = (((0,), (1,)), ((), ()))
    pre_pair = lax.dot_general(near, attention, left_rows, preferred_element_type=f32)
    pre_pair = pre_pair + lax.dot_general(far, far_attention, left_rows, preferred_element_type=f32)
    mine = lax.dynamic_slice_in_dim(pre_pair, c * part, part, 0)
    other = lax.dynamic_slice_in_dim(pre_pair, (1 - c) * part, part, 0)
    pre = mine + flip_core(other.astype(bf16)).astype(f32)

    scaled = cotangent.T.astype(f32) * gain
    stats = jnp.stack([jnp.sum(pre * pre, axis=0), jnp.sum(scaled * pre, axis=0)])
    stats = stats + flip_core(stats)
    stats = stats + flip_z(stats, 1, 0)
    inv_rms = lax.rsqrt(stats[0] / full_width + norm_eps)[None, :]
    proj = (stats[1] / full_width)[None, :]
    layer_out = (residual.T.astype(f32) + gain * (pre * inv_rms)).astype(bf16).T
    pre_grad = (inv_rms * scaled - pre * inv_rms**3 * proj).astype(bf16)
    peer_grad = flip_core(pre_grad)

    pair = jnp.stack([pre_grad, peer_grad])
    pair = jnp.concatenate(
        [lax.dynamic_index_in_dim(pair, c ^ j, 0, keepdims=False) for j in range(2)]
    )

    left = jnp.concatenate([attention, far_attention], axis=1)
    left = (left.astype(f32) * counted_flag).astype(bf16).T
    left = lax.optimization_barrier(left)
    s_, dz_, t_, slot_ = jnp.meshgrid(*(jnp.arange(n) for n in (4, 2, 4, 2)), indexing="ij")
    first_at = (spot + s_) % 4
    second_at = (spot_second + t_) % 4
    x_at = jnp.where(c == 0, first_at, second_at)
    y_at = jnp.where(c == 0, second_at, first_at)
    rows = slot_ * 512 + (((zh ^ dz_) * 4 + y_at) * 4 + x_at) * 16
    rows = rows.reshape(4, 2, 8).astype(jnp.int32)
    early = jnp.concatenate([rows[2, 1], rows[3, 1], rows[2, 0], rows[1, 0]])
    later = jnp.concatenate([rows[1, 1], rows[0, 1], rows[3, 0], rows[0, 0]])
    two_far, three_far, two_near, one_near = gradient_pieces(early, left, pair)
    one_far, none_far, three_near, none_near = gradient_pieces(later, left, pair)

    passing_up, from_above = along_first(two_far, 1), along_first(three_far, -1)
    passing_down, from_below = along_first(two_near, -1), along_first(one_near, 1)
    summed_below = along_first((one_far.astype(f32) + passing_up.astype(f32)).astype(bf16), 1)
    summed_above = along_first((three_near.astype(f32) + passing_down.astype(f32)).astype(bf16), -1)

    def second_sum(total):
        total = total.astype(bf16).reshape(4, 2, 16, half)
        got = [along_second(total[t], t) for t in (2, 1, 3)]
        final = total[0].astype(f32)
        for one in got:
            final = final + one.astype(f32)
        return final.astype(bf16)

    far_rows = second_sum(none_far.astype(f32) + from_above.astype(f32) + summed_below.astype(f32))
    got = [flip_z(far_rows[0], 0, 1), flip_z(far_rows[1], 1, 1)]
    near_rows = second_sum(none_near.astype(f32) + from_below.astype(f32) + summed_above.astype(f32))
    own_columns = near_rows[0].astype(f32) + got[0].astype(f32)
    far_columns = flip_z(near_rows[1], 1, 0).astype(f32) + got[1].astype(f32)
    owned_sum = jnp.where(
        zl == 0,
        jnp.concatenate([own_columns, far_columns], axis=1),
        jnp.concatenate([far_columns, own_columns], axis=1),
    )

    mean_grad = (owned_sum / counted.shape[0])[None, :, :]
    new_moment = beta_one * moment + (1.0 - beta_one) * mean_grad
    new_second = beta_two * second + (1.0 - beta_two) * mean_grad * mean_grad
    update = (
        new_moment
        / (1.0 - beta_one**step_number)
        / (jnp.sqrt(new_second / (1.0 - beta_two**step_number)) + adam_eps)
    )
    new_master = master - learn_rate * (update + weight_decay * master)

    own = new_master.astype(bf16)
    other = flip_z(own, 0, 1)
    low = jnp.concatenate([own] + [along_second(own, t) for t in (1, 2, 3)])
    low_below, low_above = along_first(low, 1), along_first(low, -1)
    high = jnp.concatenate([other] + [along_second(other, t) for t in (1, 2, 3)])
    high_below, high_above = along_first(high, 1), along_first(high, -1)
    low_far, high_far = along_first(low_below, 1), along_first(high_above, -1)
    s_, dz_, t_ = jnp.meshgrid(*(jnp.arange(n) for n in (4, 2, 4)), indexing="ij")
    first_at = (spot - s_) % 4
    second_at = (spot_second - t_) % 4
    x_at = jnp.where(c == 0, first_at, second_at)
    y_at = jnp.where(c == 0, second_at, first_at)
    rows = ((((zh ^ dz_) * 4 + y_at) * 4 + x_at) * 16).reshape(4, 8).astype(jnp.int32)
    first_rows = jnp.concatenate([rows[0], rows[1], rows[3]])
    new_proj = place_rows(first_rows, [low, high, low_below, high_below, low_above, high_above])
    new_proj = place_rows(rows[2], [low_far, high_far], new_proj)

    pair, _ = lax.optimization_barrier((pair, none_near))
    to_heads = (((0,), (1,)), ((), ()))
    attn_far = lax.dot_general(pair, far, to_heads, preferred_element_type=f32).astype(bf16)
    attn_near = lax.dot_general(pair, near, to_heads, preferred_element_type=f32)
    attn_grad = (attn_near + flip_z(attn_far, 1, 0).astype(f32)).astype(bf16)
    return (layer_out, attn_grad, new_proj, new_master, new_moment, new_second)


def solution(mesh):
    wide = Mesh(mesh.devices.reshape(sizes), axes)
    dp, mp = ("zh", "y", "x"), ("zl", "c")
    return jax.shard_map(
        local,
        mesh=wide,
        in_specs=(
            P(dp, mp),
            P(mp, None),
            P(),
            P(dp, mp),
            P(dp, mp),
            P(),
            P(mp, dp, None),
            P(mp, dp, None),
            P(mp, dp, None),
        ),
        out_specs=(
            P(dp, mp),
            P(dp, mp),
            P(mp, None),
            P(mp, dp, None),
            P(mp, dp, None),
            P(mp, dp, None),
        ),
        check_vma=False,
    )
```

```python
import jax
import jax.numpy as jnp
from jax import lax
from jax.experimental import pallas as pl
from jax.experimental.pallas import tpu as pltpu
from jax.sharding import Mesh, PartitionSpec as P

norm_eps = 1e-06
beta_one = 0.9
beta_two = 0.999
adam_eps = 1e-08
learn_rate = 0.01
weight_decay = 0.1
step_number = 100.0

axes = ("zh", "y", "x", "zl", "c")
sizes = (2, 4, 4, 2, 2)
bf16 = jnp.bfloat16
f32 = jnp.float32

places = [
    (zh, y, x, zl, c)
    for zh in range(2)
    for y in range(4)
    for x in range(4)
    for zl in range(2)
    for c in range(2)
]


def move(value, target):
    def flat(place):
        index = 0
        for size, at in zip(sizes, place):
            index = index * size + at % size
        return index

    return lax.ppermute(value, axes, [(flat(p), flat(target(*p))) for p in places])


def along_first(value, step):
    return move(
        value,
        lambda zh, y, x, zl, c: (zh, y, x + step, zl, c) if c == 0 else (zh, y + step, x, zl, c),
    )


def along_second(value, step):
    return move(
        value,
        lambda zh, y, x, zl, c: (zh, y + step, x, zl, c) if c == 0 else (zh, y, x + step, zl, c),
    )


def flip_core(value):
    return move(value, lambda zh, y, x, zl, c: (zh, y, x, zl, 1 - c))


def flip_z(value, low, high):
    return move(value, lambda zh, y, x, zl, c: (zh ^ high, y, x, zl ^ low, c))


def gradient_kernel(rows_ref, left_ref, right_ref, *rest):
    outs, sent = rest[:4], rest[4]

    @pl.when(pl.program_id(0) == 0)
    def _():
        for k in range(32):
            row = pl.multiple_of(rows_ref[k], 16)
            sent[pl.ds(16 * k, 16), :] = left_ref[pl.ds(row, 16), :]

    term = lax.dot_general(
        sent[...], right_ref[...], (((1,), (1,)), ((), ())), preferred_element_type=f32
    )
    term = term.astype(bf16).reshape(4, 8, 16, right_ref.shape[0])
    for one in range(4):
        outs[one][...] = term[one]


def gradient_pieces(rows, left, right):
    heads, tokens = left.shape
    columns = right.shape[0]
    width = 896
    return pl.pallas_call(
        gradient_kernel,
        grid_spec=pltpu.PrefetchScalarGridSpec(
            num_scalar_prefetch=1,
            grid=(columns // width,),
            in_specs=[
                pl.BlockSpec((heads, tokens), lambda i, rows: (0, 0)),
                pl.BlockSpec((width, tokens), lambda i, rows: (i, 0)),
            ],
            out_specs=[pl.BlockSpec((8, 16, width), lambda i, rows: (0, 0, i))] * 4,
            scratch_shapes=[pltpu.VMEM((512, tokens), bf16)],
        ),
        out_shape=[jax.ShapeDtypeStruct((8, 16, columns), bf16)] * 4,
        compiler_params=pltpu.CompilerParams(vmem_limit_bytes=24 * 1024 * 1024),
        cost_estimate=pl.CostEstimate(
            flops=2 * 512 * tokens * columns, bytes_accessed=6_000_000, transcendentals=0
        ),
    )(rows, left, right)


def whole(kernel, operands, outs, limit, flops=0, loose=(), scalars=()):
    vmem = pl.BlockSpec(memory_space=pltpu.VMEM)

    def body(*refs):
        count = len(scalars) + len(operands)
        kernel(*refs[:count], *refs[count + len(loose) :])

    moved = sum(2 * v.size for v in operands)
    return pl.pallas_call(
        body,
        in_specs=[pl.BlockSpec(memory_space=pltpu.SMEM)] * len(scalars)
        + [vmem] * len(operands)
        + [pl.BlockSpec(memory_space=pl.ANY)] * len(loose),
        out_specs=[vmem] * len(outs),
        out_shape=[jax.ShapeDtypeStruct(shape, dtype) for shape, dtype in outs],
        compiler_params=pltpu.CompilerParams(vmem_limit_bytes=limit * 1024 * 1024),
        cost_estimate=pl.CostEstimate(flops=flops, bytes_accessed=moved, transcendentals=0),
    )(*scalars, *operands, *loose)


def join_kernel(*refs):
    *pieces, low_ref, high_ref = refs
    for t in range(4):
        low_ref[t : t + 1] = pieces[t][...]
        high_ref[t : t + 1] = pieces[4 + t][...]


def place_kernel(rows_ref, *refs):
    *pieces, out_ref, sems = refs
    copies = [
        pltpu.make_async_copy(
            piece.at[k],
            out_ref.at[pl.ds(pl.multiple_of(rows_ref[4 * i + k], 16), 16)],
            sems.at[4 * i + k],
        )
        for i, piece in enumerate(pieces)
        for k in range(4)
    ]
    for copy in copies:
        copy.start()
    for copy in copies:
        copy.wait()


def place_more_kernel(rows_ref, earlier_ref, *refs):
    place_kernel(rows_ref, *refs)


def place_rows(rows, pieces, earlier=None):
    count = len(pieces)
    anywhere = pl.BlockSpec(memory_space=pl.ANY)
    before = [] if earlier is None else [earlier]
    return pl.pallas_call(
        place_more_kernel if before else place_kernel,
        grid_spec=pltpu.PrefetchScalarGridSpec(
            num_scalar_prefetch=1,
            grid=(1,),
            in_specs=[anywhere] * len(before) + [pl.BlockSpec(memory_space=pltpu.VMEM)] * count,
            out_specs=anywhere,
            scratch_shapes=[pltpu.SemaphoreType.DMA((4 * count,))],
        ),
        out_shape=jax.ShapeDtypeStruct((512, pieces[0].shape[-1]), bf16),
        input_output_aliases={1: 0} if before else {},
        compiler_params=pltpu.CompilerParams(vmem_limit_bytes=24 * 1024 * 1024),
        cost_estimate=pl.CostEstimate(
            flops=0, bytes_accessed=1_400_000 * count, transcendentals=0
        ),
    )(rows, *before, *pieces)


def local(attention, out_proj, post_gain, residual, cotangent, counted, master, moment, second):
    zh, y, x, zl, c = (lax.axis_index(a) for a in axes)
    replica = (zh * 4 + y) * 4 + x
    tokens, part = residual.shape
    heads = attention.shape[1]
    full_width = post_gain.shape[0]
    half = full_width // 2
    gain = lax.dynamic_slice_in_dim(post_gain, (zl * 2 + c) * part, part, 0)[:, None]
    counted_flag = jnp.sum((counted == replica).astype(f32))
    spot = jnp.where(c == 0, x, y)
    spot_second = jnp.where(c == 0, y, x)

    near = jnp.where(zl == 0, out_proj[:, :half], out_proj[:, half:])
    share, shared = 80, 320
    shares = lax.dynamic_slice_in_dim(out_proj, spot * share, share, 0)
    received = flip_z(jnp.where(zl == 0, shares[:, half:], shares[:, :half]), 1, 0)
    rest = out_proj[shared:]
    direct = flip_z(jnp.where(zl == 0, rest[:, half:], rest[:, :half]), 1, 1)
    far_attention = flip_z(attention, 1, 0)
    rel = jnp.stack([received] + [along_first(received, s) for s in (1, 2, 3)])
    far = jnp.concatenate(
        [lax.dynamic_index_in_dim(rel, (spot - j) % 4, 0, keepdims=False) for j in range(4)]
        + [direct]
    )

    left_rows = (((0,), (1,)), ((), ()))
    pre_pair = lax.dot_general(near, attention, left_rows, preferred_element_type=f32)
    pre_pair = pre_pair + lax.dot_general(far, far_attention, left_rows, preferred_element_type=f32)
    lower, upper = pre_pair[:part], pre_pair[part:]
    mine = jnp.where(c == 0, lower, upper)
    other = jnp.where(c == 0, upper, lower)
    mine, other = lax.optimization_barrier((mine, other.astype(bf16)))
    pre = mine + flip_core(other.astype(bf16)).astype(f32)

    scaled = cotangent.T.astype(f32) * gain
    stats = jnp.stack([jnp.sum(pre * pre, axis=0), jnp.sum(scaled * pre, axis=0)])
    stats = stats + flip_core(stats)
    stats = stats + flip_z(stats, 1, 0)
    inv_rms = lax.rsqrt(stats[0] / full_width + norm_eps)[None, :]
    proj = (stats[1] / full_width)[None, :]
    layer_out = (residual.T.astype(f32) + gain * (pre * inv_rms)).astype(bf16).T
    pre_grad = (inv_rms * scaled - pre * inv_rms**3 * proj).astype(bf16)
    peer_grad = flip_core(pre_grad)

    pair = jnp.stack([pre_grad, peer_grad])
    pair = jnp.concatenate(
        [lax.dynamic_index_in_dim(pair, c ^ j, 0, keepdims=False) for j in range(2)]
    )

    left = jnp.concatenate([attention, far_attention], axis=1)
    left = (left.astype(f32) * counted_flag).astype(bf16).T
    left = lax.optimization_barrier(left)
    s_, dz_, t_, slot_ = jnp.meshgrid(*(jnp.arange(n) for n in (4, 2, 4, 2)), indexing="ij")
    first_at = (spot + s_) % 4
    second_at = (spot_second + t_) % 4
    x_at = jnp.where(c == 0, first_at, second_at)
    y_at = jnp.where(c == 0, second_at, first_at)
    rows = slot_ * 512 + (((zh ^ dz_) * 4 + y_at) * 4 + x_at) * 16
    rows = rows.reshape(4, 2, 8).astype(jnp.int32)
    early = jnp.concatenate([rows[2, 1], rows[3, 1], rows[2, 0], rows[1, 0]])
    later = jnp.concatenate([rows[1, 1], rows[0, 1], rows[3, 0], rows[0, 0]])
    two_far, three_far, two_near, one_near = gradient_pieces(early, left, pair)
    one_far, none_far, three_near, none_near = gradient_pieces(later, left, pair)

    passing_up, from_above = along_first(two_far, 1), along_first(three_far, -1)
    passing_down, from_below = along_first(two_near, -1), along_first(one_near, 1)
    summed_below = along_first((one_far.astype(f32) + passing_up.astype(f32)).astype(bf16), 1)
    summed_above = along_first((three_near.astype(f32) + passing_down.astype(f32)).astype(bf16), -1)

    def second_sum(total):
        total = total.astype(bf16).reshape(4, 2, 16, half)
        got = [along_second(total[t], t) for t in (2, 1, 3)]
        final = total[0].astype(f32)
        for one in got:
            final = final + one.astype(f32)
        return final.astype(bf16)

    far_rows = second_sum(none_far.astype(f32) + from_above.astype(f32) + summed_below.astype(f32))
    got = [flip_z(far_rows[0], 0, 1), flip_z(far_rows[1], 1, 1)]
    near_rows = second_sum(none_near.astype(f32) + from_below.astype(f32) + summed_above.astype(f32))
    own_columns = near_rows[0].astype(f32) + got[0].astype(f32)
    far_columns = flip_z(near_rows[1], 1, 0).astype(f32) + got[1].astype(f32)
    owned_sum = jnp.where(
        zl == 0,
        jnp.concatenate([own_columns, far_columns], axis=1),
        jnp.concatenate([far_columns, own_columns], axis=1),
    )

    mean_grad = (owned_sum / counted.shape[0])[None, :, :]
    new_moment = beta_one * moment + (1.0 - beta_one) * mean_grad
    new_second = beta_two * second + (1.0 - beta_two) * mean_grad * mean_grad
    update = (
        new_moment
        / (1.0 - beta_one**step_number)
        / (jnp.sqrt(new_second / (1.0 - beta_two**step_number)) + adam_eps)
    )
    new_master = master - learn_rate * (update + weight_decay * master)

    own = new_master.astype(bf16)
    other = flip_z(own, 0, 1)
    near_blocks = [along_second(own, t) for t in (1, 2, 3)]
    peer_blocks = [along_second(other, t) for t in (1, 2, 3)]
    low, high = whole(
        join_kernel,
        [own] + near_blocks + [other] + peer_blocks,
        [((4,) + own.shape[1:], bf16)] * 2,
        16,
        loose=[],
    )
    low_below, low_above = along_first(low, 1), along_first(low, -1)
    high_below, high_above = along_first(high, 1), along_first(high, -1)
    low_far, high_far = along_first(low_below, 1), along_first(high_above, -1)
    s_, dz_, t_ = jnp.meshgrid(*(jnp.arange(n) for n in (4, 2, 4)), indexing="ij")
    first_at = (spot - s_) % 4
    second_at = (spot_second - t_) % 4
    x_at = jnp.where(c == 0, first_at, second_at)
    y_at = jnp.where(c == 0, second_at, first_at)
    rows = ((((zh ^ dz_) * 4 + y_at) * 4 + x_at) * 16).reshape(4, 8).astype(jnp.int32)
    first_rows = jnp.concatenate([rows[0], rows[1], rows[3]])
    new_proj = place_rows(first_rows, [low, high, low_below, high_below, low_above, high_above])
    new_proj = place_rows(rows[2], [low_far, high_far], new_proj)

    pair, _ = lax.optimization_barrier((pair, none_near))
    to_heads = (((0,), (1,)), ((), ()))
    attn_far = lax.dot_general(pair, far, to_heads, preferred_element_type=f32).astype(bf16)
    attn_near = lax.dot_general(pair, near, to_heads, preferred_element_type=f32)
    attn_grad = (attn_near + flip_z(attn_far, 1, 0).astype(f32)).astype(bf16)
    return (layer_out, attn_grad, new_proj, new_master, new_moment, new_second)


def solution(mesh):
    wide = Mesh(mesh.devices.reshape(sizes), axes)
    dp, mp = ("zh", "y", "x"), ("zl", "c")
    return jax.shard_map(
        local,
        mesh=wide,
        in_specs=(
            P(dp, mp),
            P(mp, None),
            P(),
            P(dp, mp),
            P(dp, mp),
            P(),
            P(mp, dp, None),
            P(mp, dp, None),
            P(mp, dp, None),
        ),
        out_specs=(
            P(dp, mp),
            P(dp, mp),
            P(mp, None),
            P(mp, dp, None),
            P(mp, dp, None),
            P(mp, dp, None),
        ),
        check_vma=False,
    )
```

```python
import jax
import jax.numpy as jnp
from jax import lax
from jax.experimental import pallas as pl
from jax.experimental.pallas import tpu as pltpu
from jax.sharding import Mesh, PartitionSpec as P

norm_eps = 1e-06
beta_one = 0.9
beta_two = 0.999
adam_eps = 1e-08
learn_rate = 0.01
weight_decay = 0.1
step_number = 100.0

axes = ("zh", "y", "x", "zl", "c")
sizes = (2, 4, 4, 2, 2)
bf16 = jnp.bfloat16
f32 = jnp.float32

places = [
    (zh, y, x, zl, c)
    for zh in range(2)
    for y in range(4)
    for x in range(4)
    for zl in range(2)
    for c in range(2)
]


def move(value, target):
    def flat(place):
        index = 0
        for size, at in zip(sizes, place):
            index = index * size + at % size
        return index

    return lax.ppermute(value, axes, [(flat(p), flat(target(*p))) for p in places])


def along_first(value, step):
    return move(
        value,
        lambda zh, y, x, zl, c: (zh, y, x + step, zl, c) if c == 0 else (zh, y + step, x, zl, c),
    )


def along_second(value, step):
    return move(
        value,
        lambda zh, y, x, zl, c: (zh, y + step, x, zl, c) if c == 0 else (zh, y, x + step, zl, c),
    )


def flip_core(value):
    return move(value, lambda zh, y, x, zl, c: (zh, y, x, zl, 1 - c))


def flip_z(value, low, high):
    return move(value, lambda zh, y, x, zl, c: (zh ^ high, y, x, zl ^ low, c))


def gradient_kernel(rows_ref, left_ref, right_ref, *rest):
    outs, sent = rest[:4], rest[4]

    @pl.when(pl.program_id(0) == 0)
    def _():
        for k in range(32):
            row = pl.multiple_of(rows_ref[k], 16)
            sent[pl.ds(16 * k, 16), :] = left_ref[pl.ds(row, 16), :]

    term = lax.dot_general(
        sent[...], right_ref[...], (((1,), (1,)), ((), ())), preferred_element_type=f32
    )
    term = term.astype(bf16).reshape(4, 8, 16, right_ref.shape[0])
    for one in range(4):
        outs[one][...] = term[one]


def gradient_pieces(rows, left, right):
    heads, tokens = left.shape
    columns = right.shape[0]
    width = 2688
    return pl.pallas_call(
        gradient_kernel,
        grid_spec=pltpu.PrefetchScalarGridSpec(
            num_scalar_prefetch=1,
            grid=(columns // width,),
            in_specs=[
                pl.BlockSpec((heads, tokens), lambda i, rows: (0, 0)),
                pl.BlockSpec((width, tokens), lambda i, rows: (i, 0)),
            ],
            out_specs=[pl.BlockSpec((8, 16, width), lambda i, rows: (0, 0, i))] * 4,
            scratch_shapes=[pltpu.VMEM((512, tokens), bf16)],
        ),
        out_shape=[jax.ShapeDtypeStruct((8, 16, columns), bf16)] * 4,
        compiler_params=pltpu.CompilerParams(vmem_limit_bytes=24 * 1024 * 1024),
        cost_estimate=pl.CostEstimate(
            flops=2 * 512 * tokens * columns, bytes_accessed=6_000_000, transcendentals=0
        ),
    )(rows, left, right)


def whole(kernel, operands, outs, limit, flops=0, loose=(), scalars=()):
    vmem = pl.BlockSpec(memory_space=pltpu.VMEM)

    def body(*refs):
        count = len(scalars) + len(operands)
        kernel(*refs[:count], *refs[count + len(loose) :])

    moved = sum(2 * v.size for v in operands)
    return pl.pallas_call(
        body,
        in_specs=[pl.BlockSpec(memory_space=pltpu.SMEM)] * len(scalars)
        + [vmem] * len(operands)
        + [pl.BlockSpec(memory_space=pl.ANY)] * len(loose),
        out_specs=[vmem] * len(outs),
        out_shape=[jax.ShapeDtypeStruct(shape, dtype) for shape, dtype in outs],
        compiler_params=pltpu.CompilerParams(vmem_limit_bytes=limit * 1024 * 1024),
        cost_estimate=pl.CostEstimate(flops=flops, bytes_accessed=moved, transcendentals=0),
    )(*scalars, *operands, *loose)


def join_kernel(*refs):
    *pieces, low_ref, high_ref = refs
    for t in range(4):
        low_ref[t : t + 1] = pieces[t][...]
        high_ref[t : t + 1] = pieces[4 + t][...]


def place_kernel(rows_ref, *refs):
    *pieces, out_ref, sems = refs
    copies = [
        pltpu.make_async_copy(
            piece.at[k],
            out_ref.at[pl.ds(pl.multiple_of(rows_ref[4 * i + k], 16), 16)],
            sems.at[4 * i + k],
        )
        for i, piece in enumerate(pieces)
        for k in range(4)
    ]
    for copy in copies:
        copy.start()
    for copy in copies:
        copy.wait()


def place_more_kernel(rows_ref, earlier_ref, *refs):
    place_kernel(rows_ref, *refs)


def place_rows(rows, pieces, earlier=None):
    count = len(pieces)
    anywhere = pl.BlockSpec(memory_space=pl.ANY)
    before = [] if earlier is None else [earlier]
    return pl.pallas_call(
        place_more_kernel if before else place_kernel,
        grid_spec=pltpu.PrefetchScalarGridSpec(
            num_scalar_prefetch=1,
            grid=(1,),
            in_specs=[anywhere] * len(before) + [pl.BlockSpec(memory_space=pltpu.VMEM)] * count,
            out_specs=anywhere,
            scratch_shapes=[pltpu.SemaphoreType.DMA((4 * count,))],
        ),
        out_shape=jax.ShapeDtypeStruct((512, pieces[0].shape[-1]), bf16),
        input_output_aliases={1: 0} if before else {},
        compiler_params=pltpu.CompilerParams(vmem_limit_bytes=24 * 1024 * 1024),
        cost_estimate=pl.CostEstimate(
            flops=0, bytes_accessed=1_400_000 * count, transcendentals=0
        ),
    )(rows, *before, *pieces)


def local(attention, out_proj, post_gain, residual, cotangent, counted, master, moment, second):
    zh, y, x, zl, c = (lax.axis_index(a) for a in axes)
    replica = (zh * 4 + y) * 4 + x
    tokens, part = residual.shape
    heads = attention.shape[1]
    full_width = post_gain.shape[0]
    half = full_width // 2
    gain = lax.dynamic_slice_in_dim(post_gain, (zl * 2 + c) * part, part, 0)[:, None]
    counted_flag = jnp.sum((counted == replica).astype(f32))
    spot = jnp.where(c == 0, x, y)
    spot_second = jnp.where(c == 0, y, x)

    near = jnp.where(zl == 0, out_proj[:, :half], out_proj[:, half:])
    share, shared = 80, 320
    shares = lax.dynamic_slice_in_dim(out_proj, spot * share, share, 0)
    received = flip_z(jnp.where(zl == 0, shares[:, half:], shares[:, :half]), 1, 0)
    rest = out_proj[shared:]
    direct = flip_z(jnp.where(zl == 0, rest[:, half:], rest[:, :half]), 1, 1)
    far_attention = flip_z(attention, 1, 0)
    rel = jnp.stack([received] + [along_first(received, s) for s in (1, 2, 3)])
    far = jnp.concatenate(
        [lax.dynamic_index_in_dim(rel, (spot - j) % 4, 0, keepdims=False) for j in range(4)]
        + [direct]
    )

    left_rows = (((0,), (1,)), ((), ()))
    pre_pair = lax.dot_general(near, attention, left_rows, preferred_element_type=f32)
    pre_pair = pre_pair + lax.dot_general(far, far_attention, left_rows, preferred_element_type=f32)
    lower, upper = pre_pair[:part], pre_pair[part:]
    mine = jnp.where(c == 0, lower, upper)
    other = jnp.where(c == 0, upper, lower)
    mine, other = lax.optimization_barrier((mine, other.astype(bf16)))
    pre = mine + flip_core(other.astype(bf16)).astype(f32)

    scaled = cotangent.T.astype(f32) * gain
    stats = jnp.stack([jnp.sum(pre * pre, axis=0), jnp.sum(scaled * pre, axis=0)])
    stats = stats + flip_core(stats)
    stats = stats + flip_z(stats, 1, 0)
    inv_rms = lax.rsqrt(stats[0] / full_width + norm_eps)[None, :]
    proj = (stats[1] / full_width)[None, :]
    layer_out = (residual.T.astype(f32) + gain * (pre * inv_rms)).astype(bf16).T
    pre_grad = (inv_rms * scaled - pre * inv_rms**3 * proj).astype(bf16)
    peer_grad = flip_core(pre_grad)

    pair = jnp.stack([pre_grad, peer_grad])
    pair = jnp.concatenate(
        [lax.dynamic_index_in_dim(pair, c ^ j, 0, keepdims=False) for j in range(2)]
    )

    left = jnp.concatenate([attention, far_attention], axis=1)
    left = (left.astype(f32) * counted_flag).astype(bf16).T
    left = lax.optimization_barrier(left)
    s_, dz_, t_, slot_ = jnp.meshgrid(*(jnp.arange(n) for n in (4, 2, 4, 2)), indexing="ij")
    first_at = (spot + s_) % 4
    second_at = (spot_second + t_) % 4
    x_at = jnp.where(c == 0, first_at, second_at)
    y_at = jnp.where(c == 0, second_at, first_at)
    rows = slot_ * 512 + (((zh ^ dz_) * 4 + y_at) * 4 + x_at) * 16
    rows = rows.reshape(4, 2, 8).astype(jnp.int32)
    early = jnp.concatenate([rows[2, 1], rows[3, 1], rows[2, 0], rows[1, 0]])
    later = jnp.concatenate([rows[1, 1], rows[0, 1], rows[3, 0], rows[0, 0]])
    two_far, three_far, two_near, one_near = gradient_pieces(early, left, pair)
    one_far, none_far, three_near, none_near = gradient_pieces(later, left, pair)

    passing_up, from_above = along_first(two_far, 1), along_first(three_far, -1)
    passing_down, from_below = along_first(two_near, -1), along_first(one_near, 1)
    summed_below = along_first((one_far.astype(f32) + passing_up.astype(f32)).astype(bf16), 1)
    summed_above = along_first((three_near.astype(f32) + passing_down.astype(f32)).astype(bf16), -1)

    def second_sum(total):
        total = total.astype(bf16).reshape(4, 2, 16, half)
        got = [along_second(total[t], t) for t in (2, 1, 3)]
        final = total[0].astype(f32)
        for one in got:
            final = final + one.astype(f32)
        return final.astype(bf16)

    far_rows = second_sum(none_far.astype(f32) + from_above.astype(f32) + summed_below.astype(f32))
    got = [flip_z(far_rows[0], 0, 1), flip_z(far_rows[1], 1, 1)]
    near_rows = second_sum(none_near.astype(f32) + from_below.astype(f32) + summed_above.astype(f32))
    own_columns = near_rows[0].astype(f32) + got[0].astype(f32)
    far_columns = flip_z(near_rows[1], 1, 0).astype(f32) + got[1].astype(f32)
    owned_sum = jnp.where(
        zl == 0,
        jnp.concatenate([own_columns, far_columns], axis=1),
        jnp.concatenate([far_columns, own_columns], axis=1),
    )

    mean_grad = (owned_sum / counted.shape[0])[None, :, :]
    new_moment = beta_one * moment + (1.0 - beta_one) * mean_grad
    new_second = beta_two * second + (1.0 - beta_two) * mean_grad * mean_grad
    update = (
        new_moment
        / (1.0 - beta_one**step_number)
        / (jnp.sqrt(new_second / (1.0 - beta_two**step_number)) + adam_eps)
    )
    new_master = master - learn_rate * (update + weight_decay * master)

    own = new_master.astype(bf16)
    other = flip_z(own, 0, 1)
    near_blocks = [along_second(own, t) for t in (1, 2, 3)]
    peer_blocks = [along_second(other, t) for t in (1, 2, 3)]
    low, high = whole(
        join_kernel,
        [own] + near_blocks + [other] + peer_blocks,
        [((4,) + own.shape[1:], bf16)] * 2,
        16,
        loose=[],
    )
    low_below, low_above = along_first(low, 1), along_first(low, -1)
    high_below, high_above = along_first(high, 1), along_first(high, -1)
    low_far, high_far = along_first(low_below, 1), along_first(high_above, -1)
    s_, dz_, t_ = jnp.meshgrid(*(jnp.arange(n) for n in (4, 2, 4)), indexing="ij")
    first_at = (spot - s_) % 4
    second_at = (spot_second - t_) % 4
    x_at = jnp.where(c == 0, first_at, second_at)
    y_at = jnp.where(c == 0, second_at, first_at)
    rows = ((((zh ^ dz_) * 4 + y_at) * 4 + x_at) * 16).reshape(4, 8).astype(jnp.int32)
    first_rows = jnp.concatenate([rows[0], rows[1], rows[3]])
    new_proj = place_rows(first_rows, [low, high, low_below, high_below, low_above, high_above])
    new_proj = place_rows(rows[2], [low_far, high_far], new_proj)

    pair, _ = lax.optimization_barrier((pair, none_near))
    to_heads = (((0,), (1,)), ((), ()))
    attn_far = lax.dot_general(pair, far, to_heads, preferred_element_type=f32).astype(bf16)
    attn_near = lax.dot_general(pair, near, to_heads, preferred_element_type=f32)
    attn_grad = (attn_near + flip_z(attn_far, 1, 0).astype(f32)).astype(bf16)
    return (layer_out, attn_grad, new_proj, new_master, new_moment, new_second)


def solution(mesh):
    wide = Mesh(mesh.devices.reshape(sizes), axes)
    dp, mp = ("zh", "y", "x"), ("zl", "c")
    return jax.shard_map(
        local,
        mesh=wide,
        in_specs=(
            P(dp, mp),
            P(mp, None),
            P(),
            P(dp, mp),
            P(dp, mp),
            P(),
            P(mp, dp, None),
            P(mp, dp, None),
            P(mp, dp, None),
        ),
        out_specs=(
            P(dp, mp),
            P(dp, mp),
            P(mp, None),
            P(mp, dp, None),
            P(mp, dp, None),
            P(mp, dp, None),
        ),
        check_vma=False,
    )
```

```python
import jax
import jax.numpy as jnp
from jax import lax
from jax.experimental import pallas as pl
from jax.experimental.pallas import tpu as pltpu
from jax.sharding import Mesh, PartitionSpec as P

norm_eps = 1e-06
beta_one = 0.9
beta_two = 0.999
adam_eps = 1e-08
learn_rate = 0.01
weight_decay = 0.1
step_number = 100.0

axes = ("zh", "y", "x", "zl", "c")
sizes = (2, 4, 4, 2, 2)
bf16 = jnp.bfloat16
f32 = jnp.float32

places = [
    (zh, y, x, zl, c)
    for zh in range(2)
    for y in range(4)
    for x in range(4)
    for zl in range(2)
    for c in range(2)
]


def move(value, target):
    def flat(place):
        index = 0
        for size, at in zip(sizes, place):
            index = index * size + at % size
        return index

    return lax.ppermute(value, axes, [(flat(p), flat(target(*p))) for p in places])


def along_first(value, step):
    return move(
        value,
        lambda zh, y, x, zl, c: (zh, y, x + step, zl, c) if c == 0 else (zh, y + step, x, zl, c),
    )


def along_second(value, step):
    return move(
        value,
        lambda zh, y, x, zl, c: (zh, y + step, x, zl, c) if c == 0 else (zh, y, x + step, zl, c),
    )


def flip_core(value):
    return move(value, lambda zh, y, x, zl, c: (zh, y, x, zl, 1 - c))


def flip_z(value, low, high):
    return move(value, lambda zh, y, x, zl, c: (zh ^ high, y, x, zl ^ low, c))


def gradient_kernel(rows_ref, left_ref, right_ref, *rest):
    outs, sent = rest[:4], rest[4]

    @pl.when(pl.program_id(0) == 0)
    def _():
        for k in range(32):
            row = pl.multiple_of(rows_ref[k], 16)
            sent[pl.ds(16 * k, 16), :] = left_ref[pl.ds(row, 16), :]

    term = lax.dot_general(
        sent[...], right_ref[...], (((1,), (1,)), ((), ())), preferred_element_type=f32
    )
    term = term.astype(bf16).reshape(4, 8, 16, right_ref.shape[0])
    for one in range(4):
        outs[one][...] = term[one]


def gradient_pieces(rows, left, right):
    heads, tokens = left.shape
    columns = right.shape[0]
    width = 2688
    return pl.pallas_call(
        gradient_kernel,
        grid_spec=pltpu.PrefetchScalarGridSpec(
            num_scalar_prefetch=1,
            grid=(columns // width,),
            in_specs=[
                pl.BlockSpec((heads, tokens), lambda i, rows: (0, 0)),
                pl.BlockSpec((width, tokens), lambda i, rows: (i, 0)),
            ],
            out_specs=[pl.BlockSpec((8, 16, width), lambda i, rows: (0, 0, i))] * 4,
            scratch_shapes=[pltpu.VMEM((512, tokens), bf16)],
        ),
        out_shape=[jax.ShapeDtypeStruct((8, 16, columns), bf16)] * 4,
        compiler_params=pltpu.CompilerParams(vmem_limit_bytes=24 * 1024 * 1024),
        cost_estimate=pl.CostEstimate(
            flops=2 * 512 * tokens * columns, bytes_accessed=6_000_000, transcendentals=0
        ),
    )(rows, left, right)


def whole(kernel, operands, outs, limit, flops=0, loose=(), scalars=()):
    vmem = pl.BlockSpec(memory_space=pltpu.VMEM)

    def body(*refs):
        count = len(scalars) + len(operands)
        kernel(*refs[:count], *refs[count + len(loose) :])

    moved = sum(2 * v.size for v in operands)
    return pl.pallas_call(
        body,
        in_specs=[pl.BlockSpec(memory_space=pltpu.SMEM)] * len(scalars)
        + [vmem] * len(operands)
        + [pl.BlockSpec(memory_space=pl.ANY)] * len(loose),
        out_specs=[vmem] * len(outs),
        out_shape=[jax.ShapeDtypeStruct(shape, dtype) for shape, dtype in outs],
        compiler_params=pltpu.CompilerParams(vmem_limit_bytes=limit * 1024 * 1024),
        cost_estimate=pl.CostEstimate(flops=flops, bytes_accessed=moved, transcendentals=0),
    )(*scalars, *operands, *loose)


def join_kernel(*refs):
    *pieces, low_ref, high_ref = refs
    for t in range(4):
        low_ref[t : t + 1] = pieces[t][...]
        high_ref[t : t + 1] = pieces[4 + t][...]


def place_kernel(rows_ref, *refs):
    *pieces, out_ref, sems = refs
    copies = [
        pltpu.make_async_copy(
            piece.at[k],
            out_ref.at[pl.ds(pl.multiple_of(rows_ref[4 * i + k], 16), 16)],
            sems.at[4 * i + k],
        )
        for i, piece in enumerate(pieces)
        for k in range(4)
    ]
    for copy in copies:
        copy.start()
    for copy in copies:
        copy.wait()


def place_more_kernel(rows_ref, earlier_ref, *refs):
    place_kernel(rows_ref, *refs)


def place_rows(rows, pieces, earlier=None):
    count = len(pieces)
    anywhere = pl.BlockSpec(memory_space=pl.ANY)
    before = [] if earlier is None else [earlier]
    return pl.pallas_call(
        place_more_kernel if before else place_kernel,
        grid_spec=pltpu.PrefetchScalarGridSpec(
            num_scalar_prefetch=1,
            grid=(1,),
            in_specs=[anywhere] * len(before) + [pl.BlockSpec(memory_space=pltpu.VMEM)] * count,
            out_specs=anywhere,
            scratch_shapes=[pltpu.SemaphoreType.DMA((4 * count,))],
        ),
        out_shape=jax.ShapeDtypeStruct((512, pieces[0].shape[-1]), bf16),
        input_output_aliases={1: 0} if before else {},
        compiler_params=pltpu.CompilerParams(vmem_limit_bytes=24 * 1024 * 1024),
        cost_estimate=pl.CostEstimate(
            flops=0, bytes_accessed=1_400_000 * count, transcendentals=0
        ),
    )(rows, *before, *pieces)


def local(attention, out_proj, post_gain, residual, cotangent, counted, master, moment, second):
    zh, y, x, zl, c = (lax.axis_index(a) for a in axes)
    replica = (zh * 4 + y) * 4 + x
    tokens, part = residual.shape
    heads = attention.shape[1]
    full_width = post_gain.shape[0]
    half = full_width // 2
    gain = lax.dynamic_slice_in_dim(post_gain, (zl * 2 + c) * part, part, 0)[:, None]
    counted_flag = jnp.sum((counted == replica).astype(f32))
    spot = jnp.where(c == 0, x, y)
    spot_second = jnp.where(c == 0, y, x)

    near = jnp.where(zl == 0, out_proj[:, :half], out_proj[:, half:])
    share, shared = 80, 320
    wanted = lax.dynamic_slice(out_proj, (spot * share, (1 - zl) * half), (share, half))
    received = flip_z(wanted, 1, 0)
    rest = out_proj[shared:]
    direct = flip_z(jnp.where(zl == 0, rest[:, half:], rest[:, :half]), 1, 1)
    far_attention = flip_z(attention, 1, 0)
    rel = jnp.stack([received] + [along_first(received, s) for s in (1, 2, 3)])
    far = jnp.concatenate(
        [lax.dynamic_index_in_dim(rel, (spot - j) % 4, 0, keepdims=False) for j in range(4)]
        + [direct]
    )

    left_rows = (((0,), (1,)), ((), ()))
    pre_pair = lax.dot_general(near, attention, left_rows, preferred_element_type=f32)
    pre_pair = pre_pair + lax.dot_general(far, far_attention, left_rows, preferred_element_type=f32)
    lower, upper = pre_pair[:part], pre_pair[part:]
    mine = jnp.where(c == 0, lower, upper)
    other = jnp.where(c == 0, upper, lower)
    mine, other = lax.optimization_barrier((mine, other.astype(bf16)))
    pre = mine + flip_core(other.astype(bf16)).astype(f32)

    scaled = cotangent.T.astype(f32) * gain
    stats = jnp.stack([jnp.sum(pre * pre, axis=0), jnp.sum(scaled * pre, axis=0)])
    stats = stats + flip_core(stats)
    stats = stats + flip_z(stats, 1, 0)
    inv_rms = lax.rsqrt(stats[0] / full_width + norm_eps)[None, :]
    proj = (stats[1] / full_width)[None, :]
    layer_out = (residual.T.astype(f32) + gain * (pre * inv_rms)).astype(bf16).T
    pre_grad = (inv_rms * scaled - pre * inv_rms**3 * proj).astype(bf16)
    peer_grad = flip_core(pre_grad)

    pair = jnp.stack([pre_grad, peer_grad])
    pair = jnp.concatenate(
        [lax.dynamic_index_in_dim(pair, c ^ j, 0, keepdims=False) for j in range(2)]
    )

    left = jnp.concatenate([attention, far_attention], axis=1)
    left = (left.astype(f32) * counted_flag).astype(bf16).T
    left = lax.optimization_barrier(left)
    s_, dz_, t_, slot_ = jnp.meshgrid(*(jnp.arange(n) for n in (4, 2, 4, 2)), indexing="ij")
    first_at = (spot + s_) % 4
    second_at = (spot_second + t_) % 4
    x_at = jnp.where(c == 0, first_at, second_at)
    y_at = jnp.where(c == 0, second_at, first_at)
    rows = slot_ * 512 + (((zh ^ dz_) * 4 + y_at) * 4 + x_at) * 16
    rows = rows.reshape(4, 2, 8).astype(jnp.int32)
    early = jnp.concatenate([rows[2, 1], rows[3, 1], rows[2, 0], rows[1, 0]])
    later = jnp.concatenate([rows[1, 1], rows[0, 1], rows[3, 0], rows[0, 0]])
    two_far, three_far, two_near, one_near = gradient_pieces(early, left, pair)
    one_far, none_far, three_near, none_near = gradient_pieces(later, left, pair)

    passing_up, from_above = along_first(two_far, 1), along_first(three_far, -1)
    passing_down, from_below = along_first(two_near, -1), along_first(one_near, 1)
    summed_below = along_first((one_far.astype(f32) + passing_up.astype(f32)).astype(bf16), 1)
    summed_above = along_first((three_near.astype(f32) + passing_down.astype(f32)).astype(bf16), -1)

    def second_sum(total):
        total = total.astype(bf16).reshape(4, 2, 16, half)
        got = [along_second(total[t], t) for t in (2, 1, 3)]
        final = total[0].astype(f32)
        for one in got:
            final = final + one.astype(f32)
        return final.astype(bf16)

    far_rows = second_sum(none_far.astype(f32) + from_above.astype(f32) + summed_below.astype(f32))
    got = [flip_z(far_rows[0], 0, 1), flip_z(far_rows[1], 1, 1)]
    near_rows = second_sum(none_near.astype(f32) + from_below.astype(f32) + summed_above.astype(f32))
    own_columns = near_rows[0].astype(f32) + got[0].astype(f32)
    far_columns = flip_z(near_rows[1], 1, 0).astype(f32) + got[1].astype(f32)
    owned_sum = jnp.where(
        zl == 0,
        jnp.concatenate([own_columns, far_columns], axis=1),
        jnp.concatenate([far_columns, own_columns], axis=1),
    )

    mean_grad = (owned_sum / counted.shape[0])[None, :, :]
    new_moment = beta_one * moment + (1.0 - beta_one) * mean_grad
    new_second = beta_two * second + (1.0 - beta_two) * mean_grad * mean_grad
    update = (
        new_moment
        / (1.0 - beta_one**step_number)
        / (jnp.sqrt(new_second / (1.0 - beta_two**step_number)) + adam_eps)
    )
    new_master = master - learn_rate * (update + weight_decay * master)

    own = new_master.astype(bf16)
    other = flip_z(own, 0, 1)
    near_blocks = [along_second(own, t) for t in (1, 2, 3)]
    peer_blocks = [along_second(other, t) for t in (1, 2, 3)]
    low, high = whole(
        join_kernel,
        [own] + near_blocks + [other] + peer_blocks,
        [((4,) + own.shape[1:], bf16)] * 2,
        16,
        loose=[],
    )
    low_below, low_above = along_first(low, 1), along_first(low, -1)
    high_below, high_above = along_first(high, 1), along_first(high, -1)
    low_far, high_far = along_first(low_below, 1), along_first(high_above, -1)
    s_, dz_, t_ = jnp.meshgrid(*(jnp.arange(n) for n in (4, 2, 4)), indexing="ij")
    first_at = (spot - s_) % 4
    second_at = (spot_second - t_) % 4
    x_at = jnp.where(c == 0, first_at, second_at)
    y_at = jnp.where(c == 0, second_at, first_at)
    rows = ((((zh ^ dz_) * 4 + y_at) * 4 + x_at) * 16).reshape(4, 8).astype(jnp.int32)
    first_rows = jnp.concatenate([rows[0], rows[1], rows[3]])
    new_proj = place_rows(first_rows, [low, high, low_below, high_below, low_above, high_above])
    new_proj = place_rows(rows[2], [low_far, high_far], new_proj)

    pair, _ = lax.optimization_barrier((pair, none_near))
    to_heads = (((0,), (1,)), ((), ()))
    attn_far = lax.dot_general(pair, far, to_heads, preferred_element_type=f32).astype(bf16)
    attn_near = lax.dot_general(pair, near, to_heads, preferred_element_type=f32)
    attn_grad = (attn_near + flip_z(attn_far, 1, 0).astype(f32)).astype(bf16)
    return (layer_out, attn_grad, new_proj, new_master, new_moment, new_second)


def solution(mesh):
    wide = Mesh(mesh.devices.reshape(sizes), axes)
    dp, mp = ("zh", "y", "x"), ("zl", "c")
    return jax.shard_map(
        local,
        mesh=wide,
        in_specs=(
            P(dp, mp),
            P(mp, None),
            P(),
            P(dp, mp),
            P(dp, mp),
            P(),
            P(mp, dp, None),
            P(mp, dp, None),
            P(mp, dp, None),
        ),
        out_specs=(
            P(dp, mp),
            P(dp, mp),
            P(mp, None),
            P(mp, dp, None),
            P(mp, dp, None),
            P(mp, dp, None),
        ),
        check_vma=False,
    )
```
